32 devices in a mesh: igrp: 4 (over x, core), jgrp: 8 (over z, y).
Axes of the slice: x: 2, y: 2, z: 4, core: 2. Of those that a mesh axis runs over, the one named last changes fastest.
Arguments:
- t_start: bfloat16 [64, 64, 256, 256], P('igrp', 'jgrp'), may hold values from -2.390625 to 2.390625
- integrals: bfloat16 [64, 64, 256, 256], P('igrp', 'jgrp'), may hold values from -6 to 6
- weights: bfloat16 [64, 8, 256, 256], P('igrp'), may hold values from -0.125 to 0.125
- neighbours: int32 [64, 8], replicated, may hold values from 0 to 63, as said below
- eps_occ: float32 [64], replicated, may hold values from -2 to -0.5
- eps_vir: float32 [256], replicated, may hold values from 0.2 to 4
Outputs:
- amplitudes: float32 [64, 64, 256, 256], P('igrp', 'jgrp')
The draws below stay inside these ranges and needn't reach their ends.
Inputs may be any that keep to these rules, and one draw needn't show every extreme that they name: `neighbours`: the entries of a row are distinct. For every block of 16 consecutive rows starting at a multiple of 16, and every block of 16 consecutive orbitals starting at a multiple of 16, exactly 2 distinct orbitals of that block appear in those rows.
All inputs are finite; a program needn't handle non-finite values.
Results may differ from the reference program's by a relative error of at most 0.0018.
Values may be sent and summed in bfloat16 or wider, within the bound.
No kernel may reach another device: no remote copies, remote signals or barrier semaphores. Data moves between devices by JAX's collectives and lax.ppermute only.
A program may use at most 256 MiB of HBM per device.

```python
import math
import jax
import jax.numpy as jnp
from jax import lax

NOCC = 64
V = 256
NNB = 8
CAP = 2
ITERS = 2
OI_DEV = 16


def draw_neighbours(key, part):
    groups = NOCC // OI_DEV
    allowed = CAP * groups
    first_key, second_key = jax.random.split(jax.random.fold_in(key, 7))
    scores = jax.random.randint(first_key, (groups, groups, OI_DEV), 0, 2 ** 20)
    scores = scores * OI_DEV + jnp.arange(OI_DEV, dtype=jnp.int32)[None, None, :]
    chosen = jnp.argsort(scores, axis=2)[:, :, :CAP].astype(jnp.int32)
    listed = chosen + (jnp.arange(groups, dtype=jnp.int32) * OI_DEV)[None, :, None]
    listed = listed.reshape(groups, allowed)
    shuffle = jax.random.randint(second_key, (groups, allowed), 0, 2 ** 20)
    shuffle = shuffle * allowed + jnp.arange(allowed, dtype=jnp.int32)[None, :]
    ordering = jnp.argsort(shuffle, axis=1).astype(jnp.int32)
    position = (jnp.arange(OI_DEV, dtype=jnp.int32)[:, None] * NNB + jnp.arange(NNB, dtype=jnp.int32)[None, :]) % allowed

    def per_group(group_list, group_order):
        return group_list[group_order[position]]
    result = jax.vmap(per_group)(listed, ordering)
    return result.reshape(NOCC, NNB).astype(jnp.int32)


def shard_levels(own_key, dims, cuts, low, high):
    def one(dim, parts):
        steps = jax.random.uniform(jax.random.fold_in(jax.random.fold_in(own_key, 6), dim), (parts,), jnp.float32, low / len(cuts), high / len(cuts))
        return jnp.repeat(jnp.exp(steps), dims[dim] // parts).reshape((-1,) + (1,) * (len(dims) - dim - 1))

    level = one(*cuts[0])
    for cut in cuts[1:]:
        level = level * one(*cut)
    return level


def centred(rng, extent, deviation, reach, shards=(), kind=jnp.bfloat16):
    values = jax.random.normal(rng, extent, jnp.float32) * deviation
    if len(shards) > 0:
        values = shard_levels(rng, extent, shards, -0.22, 0.18) * values
    return jnp.clip(values, min=-reach, max=reach).astype(kind)


def setup_inputs(seed: int = 0) -> dict:
    seeds = jax.random.split(jax.random.key(seed), 7)
    t_start = centred(seeds[0], (NOCC, NOCC, V, V), 0.3, 2.390625, ((0, 4), (1, 8)))
    integrals = centred(seeds[1], (NOCC, NOCC, V, V), 1.0, 6.0, ((0, 4), (1, 8)))
    weights = centred(seeds[2], (NOCC, NNB, V, V), (NNB * V) ** -0.5, 0.125, ((0, 4),))
    neighbours = draw_neighbours(jax.random.fold_in(seeds[6], 71), 0)
    eps_occ = jnp.clip(jax.random.uniform(seeds[4], (NOCC,), jnp.float32, -2.0, -0.5), -2.0, -0.5)
    eps_vir = jnp.clip(jnp.exp(jax.random.uniform(seeds[5], (V,), jnp.float32, math.log(0.2), math.log(4.0))), 0.2, 4.0)
    return dict(t_start=t_start, integrals=integrals, weights=weights, neighbours=neighbours, eps_occ=eps_occ, eps_vir=eps_vir)


def cycle_product(current, weights, neighbours):
    def per_orbital(inputs):
        weight_rows, listed = inputs
        blocks = jnp.take(current, listed, axis=0)
        return jnp.einsum('mac,mjcb->jab', weight_rows.astype(jnp.float32), blocks.astype(jnp.float32))
    return lax.map(per_orbital, (weights, neighbours)).astype(jnp.bfloat16)


def reference(t_start, integrals, weights, neighbours, eps_occ, eps_vir):
    denominator = (eps_vir[None, None, :, None] + eps_vir[None, None, None, :]
                   - eps_occ[:, None, None, None] - eps_occ[None, :, None, None])
    current = t_start
    updated = t_start.astype(jnp.float32)
    for sweep in range(ITERS):
        cycle_term = cycle_product(current, weights, neighbours)
        flipped = cycle_term.transpose(1, 0, 3, 2)
        updated = (integrals.astype(jnp.float32) + cycle_term.astype(jnp.float32)
                   + flipped.astype(jnp.float32)) / denominator
        current = updated.astype(jnp.bfloat16)
    return updated
```

```python
import functools

import jax
import jax.numpy as jnp
from jax import lax
from jax.experimental import pallas as pl
from jax.experimental.pallas import tpu as pltpu
from jax.sharding import PartitionSpec as P

CAP = 2
ITERS = 2
AXES = ("igrp", "jgrp")
VMEM = 56 * 2**20
F32, BF16, I32 = jnp.float32, jnp.bfloat16, jnp.int32


def params():
    return pltpu.CompilerParams(vmem_limit_bytes=VMEM)


def cost(flops, moved):
    return pl.CostEstimate(flops=flops, bytes_accessed=moved, transcendentals=0)


def resident(shape):
    return pl.BlockSpec(shape, lambda *_: (0,) * len(shape))


def listed_offsets(neighbours, groups, rows):
    named = neighbours.reshape(groups, -1)
    every = jnp.arange(groups * rows, dtype=I32)
    flags = jnp.any(named[:, :, None] == every[None, None, :], axis=1).reshape(groups, groups, rows)
    offsets = jnp.arange(rows, dtype=I32)
    before = (offsets[:, None] < offsets[None, :]).astype(I32)
    rank = jnp.sum(flags.astype(I32)[:, :, :, None] * before[None, None], axis=2)
    hits = flags[:, :, :, None] & (rank[:, :, :, None] == jnp.arange(CAP, dtype=I32))
    return jnp.sum(hits.astype(I32) * offsets[None, None, :, None], axis=2)


def relative_slots(neighbours, lists, groups, rows):
    group = jnp.arange(groups, dtype=I32)[:, None, None]
    block = jnp.arange(groups, dtype=I32)[None, :, None]
    orbital = block * rows + lists
    slot = (group ^ block) * CAP + jnp.arange(CAP, dtype=I32)[None, None, :]
    grouped = neighbours.reshape(groups, -1)
    hits = (grouped[:, :, None, None] == orbital[:, None]).astype(I32)
    return jnp.sum(hits * slot[:, None], axis=(2, 3)).reshape(neighbours.shape)


def pick_kernel(rows_ref, *refs):
    half = len(refs) // 2
    for source, target in zip(refs[:half], refs[half:]):
        target[:, 0] = source[0]


def pick_rows(t, rows, groups):
    _, cols, v, _ = t.shape
    return pl.pallas_call(
        pick_kernel,
        out_shape=[jax.ShapeDtypeStruct((cols, CAP, v, v), t.dtype)] * groups,
        grid_spec=pltpu.PrefetchScalarGridSpec(
            num_scalar_prefetch=1,
            grid=(CAP,),
            in_specs=[
                pl.BlockSpec((1, cols, v, v), lambda c, rows, s=s: (rows[s * CAP + c], 0, 0, 0))
                for s in range(groups)
            ],
            out_specs=[pl.BlockSpec((cols, 1, v, v), lambda c, rows: (0, c, 0, 0))] * groups,
        ),
        compiler_params=params(),
        cost_estimate=cost(0, 4 * groups * CAP * cols * v * v),
        name="pick_rows",
    )(rows, *[t] * groups)


def slotted_kernel(slots_ref, w_ref, o_ref):
    listed, v = w_ref.shape[1], w_ref.shape[2]
    row = pl.program_id(0) * listed
    if o_ref.shape[2] > listed * v:
        o_ref[...] = jnp.zeros_like(o_ref)
    for m in range(listed):
        start = pl.multiple_of(slots_ref[row + m] * v, v)
        o_ref[0, :, pl.ds(start, v)] = w_ref[0, m]


def slotted(w, slots, groups):
    rows, listed, v, _ = w.shape
    depth = groups * CAP * v
    return pl.pallas_call(
        slotted_kernel,
        out_shape=jax.ShapeDtypeStruct((rows, v, depth), w.dtype),
        grid_spec=pltpu.PrefetchScalarGridSpec(
            num_scalar_prefetch=1,
            grid=(rows,),
            in_specs=[pl.BlockSpec((1, listed, v, v), lambda i, slots: (i, 0, 0, 0))],
            out_specs=pl.BlockSpec((1, v, depth), lambda i, slots: (i, 0, 0)),
        ),
        compiler_params=params(),
        cost_estimate=cost(0, 4 * rows * v * depth),
        name="slotted",
    )(slots.reshape(-1), w)


def stacked(refs, at):
    v = refs[0].shape[-1]
    return jnp.concatenate([r[at].reshape(-1, v) for r in refs], axis=0)


def direct_kernel(taken, rows_ref, *refs):
    w_refs, t_refs, o_ref = refs[:taken], refs[taken:-1], refs[-1]
    cols, v = o_ref.shape[1], o_ref.shape[2]

    def column(j, carry):
        left = jnp.concatenate([w[0] for w in w_refs], axis=0)
        product = jnp.dot(left, stacked(t_refs, j), preferred_element_type=F32).astype(BF16)
        for q in range(taken):
            o_ref[q, j] = product[q * v : (q + 1) * v]
        return carry

    lax.fori_loop(0, cols, column, 0)


def direct(wp, rows, parts):
    cols, _, v, _ = parts[0].shape
    count, depth = rows.shape[0], wp.shape[2]
    taken = 4 if count % 4 == 0 else 1
    return pl.pallas_call(
        functools.partial(direct_kernel, taken),
        out_shape=jax.ShapeDtypeStruct((count, cols, v, v), BF16),
        grid_spec=pltpu.PrefetchScalarGridSpec(
            num_scalar_prefetch=1,
            grid=(count // taken,),
            in_specs=[
                pl.BlockSpec((1, v, depth), lambda n, rows, q=q: (rows[n * taken + q], 0, 0))
                for q in range(taken)
            ]
            + [resident(p.shape) for p in parts],
            out_specs=pl.BlockSpec((taken, cols, v, v), lambda n, rows: (n, 0, 0, 0)),
        ),
        compiler_params=params(),
        cost_estimate=cost(2 * count * cols * v * v * depth, 2 * count * v * (depth + cols * v)),
        name="direct",
    )(rows, *[wp] * taken, *parts)


def finish_kernel(halves, rows_ref, where_ref, occ_ref, w_ref, c_ref, k_ref, tall_ref, wide_ref, *refs):
    o_ref, base_ref = refs[-2], refs[-1]
    t_refs = refs[:-2]
    cols, v, depth = w_ref.shape
    row = rows_ref[pl.program_id(0)]
    base_ref[...] = tall_ref[...] + wide_ref[...] - occ_ref[where_ref[0] + row]
    taken = 4 if cols % 4 == 0 else 1
    by_half = [t_refs[h::halves] for h in range(halves)]

    def work(parts):
        right = stacked(parts, 0)
        for first in range(0, cols, taken):
            left = w_ref[first : first + taken].reshape(taken * v, depth)
            product = jnp.dot(left, right, preferred_element_type=F32).astype(BF16)
            for q in range(taken):
                j = first + q
                flipped = product[q * v : (q + 1) * v].astype(F32).T
                total = k_ref[0, j].astype(F32) + c_ref[0, j].astype(F32) + flipped
                value = (total / (base_ref[...] - occ_ref[where_ref[1] + j])).astype(o_ref.dtype)
                if o_ref.shape[0] == 1:
                    o_ref[0, j] = value
                else:
                    o_ref[j, 0] = value

    if halves == 1:
        work(by_half[0])
    else:
        here = (row // cols) ^ where_ref[2]
        for h in range(halves):
            pl.when(here == h)(functools.partial(work, by_half[h]))


def kept_kernel(halves, *refs):
    finish_kernel(halves, *refs[:8], *refs[9:])


def finish(wpj, c, c_first, k, tall, wide, occ, where, rows, far, out, into=None):
    cols, v, depth = wpj.shape
    halves, groups = len(far), len(far[0])
    parts = [far[h][s] for s in range(groups) for h in range(halves)]
    part = pl.BlockSpec((1, CAP, v, v), lambda n, rows, where: (rows[n] % cols, 0, 0, 0))
    one_row = (1, cols, v, v)
    by_row = pl.BlockSpec(one_row, lambda n, rows, where: (rows[n], 0, 0, 0))
    kept = [] if into is None else [into]
    return pl.pallas_call(
        functools.partial(finish_kernel if into is None else kept_kernel, halves),
        out_shape=out,
        grid_spec=pltpu.PrefetchScalarGridSpec(
            num_scalar_prefetch=2,
            grid=(rows.shape[0],),
            in_specs=[
                pl.BlockSpec(memory_space=pltpu.SMEM),
                resident(wpj.shape),
                by_row if c_first is None else pl.BlockSpec(one_row, lambda n, rows, where: (c_first + n, 0, 0, 0)),
                by_row,
                resident(tall.shape),
                resident(wide.shape),
            ]
            + [pl.BlockSpec(memory_space=pl.ANY)] * len(kept)
            + [part] * len(parts),
            out_specs=by_row
            if out.dtype == F32
            else pl.BlockSpec((cols, 1, v, v), lambda n, rows, where: (0, n, 0, 0)),
            scratch_shapes=[pltpu.VMEM((v, v), F32)],
        ),
        input_output_aliases={} if into is None else {8: 0},
        compiler_params=params(),
        cost_estimate=cost(2 * rows.shape[0] * cols * v * v * depth, 2 * cols * v * (depth + rows.shape[0] * v * 5)),
        name="finish",
    )(rows, where, occ, wpj, c, k, tall, wide, *kept, *parts)


def exchange(groups, ratio, jgroups, mine):
    near = [mine[0]] + [
        lax.ppermute(mine[s], "igrp", [(i, i ^ s) for i in range(groups)]) for s in range(1, groups)
    ]
    first = [
        lax.ppermute(
            mine[s],
            AXES,
            [
                (i * jgroups + z * ratio + y, z * jgroups + (i ^ s) * ratio + y)
                for i in range(groups)
                for z in range(groups)
                for y in range(ratio)
            ],
        )
        for s in range(groups)
    ]
    far = [first] + [
        [lax.ppermute(f, "jgrp", [(j, j ^ d) for j in range(jgroups)]) for f in first] for d in range(1, ratio)
    ]
    return near, far


def spread_weights(w, groups, ratio, jgroups, my_i, my_z):
    held = [0]
    bit = groups // 2
    while bit:
        pairs = [
            (((z ^ h) * jgroups + z * ratio + y), ((z ^ h ^ bit) * jgroups + z * ratio + y))
            for h in held
            for z in range(groups)
            for y in range(ratio)
        ]
        came = lax.ppermute(w, AXES, pairs)
        fresh = functools.reduce(jnp.logical_or, [(my_i ^ my_z) == (h ^ bit) for h in held])
        w = jnp.where(fresh, came, w)
        held = held + [h ^ bit for h in held]
        bit //= 2
    return w


def body(t_start, integrals, weights, neighbours, eps_occ, eps_vir):
    row_count, cols, v, _ = t_start.shape
    groups, jgroups = lax.axis_size("igrp"), lax.axis_size("jgrp")
    ratio = jgroups // groups
    my_i, my_j = lax.axis_index("igrp"), lax.axis_index("jgrp")
    my_z, my_half = my_j // ratio, my_j % ratio

    lists = listed_offsets(neighbours, groups, row_count)
    slots = relative_slots(neighbours, lists, groups, row_count)
    asked = lax.dynamic_slice_in_dim(lists, my_i, 1, 1)[:, 0]
    order = my_i ^ jnp.arange(groups, dtype=I32)
    rows = jnp.sum(
        asked[None] * (jnp.arange(groups, dtype=I32)[None, :, None] == order[:, None, None]).astype(I32), axis=1
    ).reshape(-1)
    every_row = jnp.arange(row_count, dtype=I32)
    where = jnp.stack([my_i * row_count, my_j * cols, my_half]).astype(I32)
    tall, wide = eps_vir.reshape(v, 1), eps_vir.reshape(1, v)

    mine = pick_rows(t_start, rows, groups)
    half_w = lax.dynamic_slice_in_dim(weights, my_half * cols, cols, 0)
    wj = spread_weights(half_w, groups, ratio, jgroups, my_i, my_z)
    wp = slotted(weights, lax.dynamic_slice_in_dim(slots, my_i * row_count, row_count, 0), groups)
    wpj = slotted(wj, lax.dynamic_slice_in_dim(slots, my_j * cols, cols, 0), groups)

    for sweep in range(ITERS - 1):
        near, far = exchange(groups, ratio, jgroups, mine)
        c = direct(wp, rows, near)
        mine = [
            finish(
                wpj, c, s * CAP, integrals, tall, wide, eps_occ, where, rows[s * CAP : (s + 1) * CAP], far,
                jax.ShapeDtypeStruct((cols, CAP, v, v), BF16),
            )
            for s in range(groups)
        ]
    near, far = exchange(groups, ratio, jgroups, mine)
    c = direct(wp, every_row, near)
    updated = None
    for d in range(ratio):
        half_rows = (my_half ^ d) * cols + jnp.arange(cols, dtype=I32)
        updated = finish(
            wpj, c, None, integrals, tall, wide, eps_occ, where, half_rows, far[d : d + 1],
            jax.ShapeDtypeStruct((row_count, cols, v, v), F32), updated,
        )
    return updated


def solution(mesh):
    placed = (
        P("igrp", "jgrp", None, None),
        P("igrp", "jgrp", None, None),
        P("igrp", None, None, None),
        P(),
        P(),
        P(),
    )
    return jax.shard_map(
        body, mesh=mesh, in_specs=placed, out_specs=P("igrp", "jgrp", None, None), check_vma=False
    )
```

```python
import functools

import jax
import jax.numpy as jnp
from jax import lax
from jax.experimental import pallas as pl
from jax.experimental.pallas import tpu as pltpu
from jax.sharding import PartitionSpec as P

CAP = 2
ITERS = 2
AXES = ("igrp", "jgrp")
VMEM = 56 * 2**20
F32, BF16, I32 = jnp.float32, jnp.bfloat16, jnp.int32


def params():
    return pltpu.CompilerParams(vmem_limit_bytes=VMEM)


def cost(flops, moved):
    return pl.CostEstimate(flops=flops, bytes_accessed=moved, transcendentals=0)


def resident(shape):
    return pl.BlockSpec(shape, lambda *_: (0,) * len(shape))


def listed_offsets(neighbours, groups, rows):
    named = neighbours.reshape(groups, -1)
    every = jnp.arange(groups * rows, dtype=I32)
    flags = jnp.any(named[:, :, None] == every[None, None, :], axis=1).reshape(groups, groups, rows)
    offsets = jnp.arange(rows, dtype=I32)
    before = (offsets[:, None] < offsets[None, :]).astype(I32)
    rank = jnp.sum(flags.astype(I32)[:, :, :, None] * before[None, None], axis=2)
    hits = flags[:, :, :, None] & (rank[:, :, :, None] == jnp.arange(CAP, dtype=I32))
    return jnp.sum(hits.astype(I32) * offsets[None, None, :, None], axis=2)


def relative_slots(neighbours, lists, groups, rows):
    group = jnp.arange(groups, dtype=I32)[:, None, None]
    block = jnp.arange(groups, dtype=I32)[None, :, None]
    orbital = block * rows + lists
    slot = (group ^ block) * CAP + jnp.arange(CAP, dtype=I32)[None, None, :]
    grouped = neighbours.reshape(groups, -1)
    hits = (grouped[:, :, None, None] == orbital[:, None]).astype(I32)
    return jnp.sum(hits * slot[:, None], axis=(2, 3)).reshape(neighbours.shape)


def pick_kernel(rows_ref, *refs):
    half = len(refs) // 2
    for source, target in zip(refs[:half], refs[half:]):
        target[:, 0] = source[0]


def pick_rows(t, rows, groups, width, chunk):
    v = t.shape[-1]
    return pl.pallas_call(
        pick_kernel,
        out_shape=[jax.ShapeDtypeStruct((width, CAP, v, v), t.dtype)] * groups,
        grid_spec=pltpu.PrefetchScalarGridSpec(
            num_scalar_prefetch=1,
            grid=(CAP,),
            in_specs=[
                pl.BlockSpec((1, width, v, v), lambda c, rows, s=s: (rows[s * CAP + c], chunk, 0, 0))
                for s in range(groups)
            ],
            out_specs=[pl.BlockSpec((width, 1, v, v), lambda c, rows: (0, c, 0, 0))] * groups,
        ),
        compiler_params=params(),
        cost_estimate=cost(0, 4 * groups * CAP * width * v * v),
        name="pick_rows",
    )(rows, *[t] * groups)


def tie_kernel(*refs):
    pass


def tie(arrays, earlier):
    if not arrays:
        return arrays
    known = {id(x) for x in arrays}
    earlier = [x for x in earlier if id(x) not in known]
    return pl.pallas_call(
        tie_kernel,
        out_shape=[jax.ShapeDtypeStruct(x.shape, x.dtype) for x in arrays],
        in_specs=[pl.BlockSpec(memory_space=pl.ANY)] * (len(arrays) + len(earlier)),
        out_specs=[pl.BlockSpec(memory_space=pl.ANY)] * len(arrays),
        input_output_aliases={n: n for n in range(len(arrays))},
        name="tie",
    )(*arrays, *earlier)


def slotted_kernel(slots_ref, pick_ref, *refs):
    w_refs, o_ref = refs[:-1], refs[-1]
    listed, v = w_refs[0].shape[1], w_refs[0].shape[2]
    row = pl.program_id(0) * listed
    if o_ref.shape[2] > listed * v:
        o_ref[...] = jnp.zeros_like(o_ref)

    def place(w_ref):
        for m in range(listed):
            start = pl.multiple_of(slots_ref[row + m] * v, v)
            o_ref[0, :, pl.ds(start, v)] = w_ref[0, m]

    for n, w_ref in enumerate(w_refs):
        pl.when(pick_ref[0] == n)(functools.partial(place, w_ref))


def slotted(sources, pick, slots, groups):
    rows, listed, v, _ = sources[0].shape
    depth = groups * CAP * v
    return pl.pallas_call(
        slotted_kernel,
        out_shape=jax.ShapeDtypeStruct((rows, v, depth), sources[0].dtype),
        grid_spec=pltpu.PrefetchScalarGridSpec(
            num_scalar_prefetch=2,
            grid=(rows,),
            in_specs=[pl.BlockSpec((1, listed, v, v), lambda i, slots, pick: (i, 0, 0, 0))] * len(sources),
            out_specs=pl.BlockSpec((1, v, depth), lambda i, slots, pick: (i, 0, 0)),
        ),
        compiler_params=params(),
        cost_estimate=cost(0, 4 * rows * v * depth),
        name="slotted",
    )(slots.reshape(-1), jnp.reshape(pick, (1,)).astype(I32), *sources)


def stacked(refs, at):
    v = refs[0].shape[-1]
    return jnp.concatenate([r[at].reshape(-1, v) for r in refs], axis=0)


def direct_kernel(taken, rows_ref, *refs):
    w_refs, t_refs, o_ref = refs[:taken], refs[taken:-1], refs[-1]
    cols, v = o_ref.shape[1], o_ref.shape[2]

    def column(j, carry):
        left = jnp.concatenate([w[0] for w in w_refs], axis=0)
        product = jnp.dot(left, stacked(t_refs, j), preferred_element_type=F32).astype(BF16)
        for q in range(taken):
            o_ref[q, j] = product[q * v : (q + 1) * v]
        return carry

    lax.fori_loop(0, cols, column, 0)


def direct(wp, rows, parts, placed=False):
    cols, _, v, _ = parts[0].shape
    count, depth = rows.shape[0], wp.shape[2]
    taken = cols if placed else 4 if count % 4 == 0 else 1
    return pl.pallas_call(
        functools.partial(direct_kernel, taken),
        out_shape=jax.ShapeDtypeStruct((wp.shape[0] if placed else count, cols, v, v), BF16),
        grid_spec=pltpu.PrefetchScalarGridSpec(
            num_scalar_prefetch=1,
            grid=(count // taken,),
            in_specs=[
                pl.BlockSpec((1, v, depth), lambda n, rows, q=q: (rows[n * taken + q], 0, 0))
                for q in range(taken)
            ]
            + [resident(p.shape) for p in parts],
            out_specs=pl.BlockSpec(
                (taken, cols, v, v), lambda n, rows: (rows[n * taken] // taken if placed else n, 0, 0, 0)
            ),
        ),
        compiler_params=params(),
        cost_estimate=cost(2 * count * cols * v * v * depth, 2 * count * v * (depth + cols * v)),
        name="direct",
    )(rows, *[wp] * taken, *parts)


def finish_kernel(sets, rows_ref, crows_ref, where_ref, held_ref, use_ref, occ_ref, tall_ref, wide_ref, *refs):
    (spans, groups), choices, outs, flip = sets
    base_ref, right_ref, made_ref = refs[-3:]
    o_refs = refs[-3 - outs : -3]
    w_refs, refs = refs[:spans], refs[spans:]
    if not flip:
        c_refs, k_refs, refs = refs[:spans], refs[spans : 2 * spans], refs[2 * spans :]
    t_refs = refs[: choices * groups]
    width, v, depth = w_refs[0].shape
    step = pl.program_id(0)
    if not flip:
        base_ref[...] = tall_ref[...] + wide_ref[...] - occ_ref[where_ref[0] + rows_ref[step]]

    def load(first):
        for s in range(groups):
            piece = t_refs[first * groups + s][0].reshape(CAP * v, v)
            right_ref[s * CAP * v : (s + 1) * CAP * v] = piece

    if choices > 1:
        for n in range(choices):
            pl.when(use_ref[step] == n)(functools.partial(load, n))
    for n in range(spans):
        left = w_refs[n][...].reshape(width * v, depth)
        right = right_ref[...] if choices > 1 else stacked(t_refs, 0)
        product = jnp.dot(left, right, preferred_element_type=F32).astype(BF16)
        for j in range(width):
            value = product[j * v : (j + 1) * v].astype(F32).T
            if not flip:
                total = k_refs[n][0, j].astype(F32) + c_refs[n][0, j].astype(F32) + value
                column = where_ref[1] + where_ref[3] + n * width + j
                value = total / (base_ref[...] - occ_ref[column])
            value = value.astype(o_refs[0].dtype)
            if outs > 1:
                made_ref[j] = value
            else:
                o_refs[0][0, n * width + j] = value

    def store(o_ref):
        o_ref[:, 0] = made_ref[...]

    if outs > 1:
        for p in range(outs):
            pl.when(step // CAP == p)(functools.partial(store, o_refs[p]))


def kept_kernel(sets, *refs):
    finish_kernel(sets, *refs[:8], *refs[9:])


def finish(w, c, crows, chunks, k, tall, wide, occ, where, rows, use, far, out, into=None):
    w = [w[h] for h in chunks]
    width, v, depth = w[0].shape
    choices, groups = len(far), len(far[0])
    parts = [t for one in far for t in one]
    spans, steps = len(chunks), rows.shape[0]
    flip = c is None
    where = jnp.concatenate([where, jnp.full((1,), chunks[0] * width, I32)])
    at = rows % width
    reads = use[None] == jnp.arange(choices, dtype=I32)[:, None]
    order = jnp.arange(steps, dtype=I32)
    gap = order[None] - order[:, None]
    rank = jnp.where(gap >= 0, gap, steps - gap)
    rank = jnp.where(reads[:, None], rank[None], 4 * steps)
    nearest = (rank == jnp.min(rank, axis=2, keepdims=True)).astype(I32)
    held = jnp.where(jnp.any(reads, axis=1)[:, None], jnp.sum(nearest * at, axis=2), 0).reshape(-1)
    part = [
        pl.BlockSpec((1, CAP, v, v), lambda n, rows, crows, where, held, use, i=i: (held[i * steps + n], 0, 0, 0))
        for i in range(choices)
        for _ in range(groups)
    ]
    one_row = (1, width, v, v)
    kept = [] if into is None else [into]
    sets = ((spans, groups), choices, len(out), flip)
    if flip:
        out_specs = [pl.BlockSpec(one_row, lambda n, *_: (n, 0, 0, 0))]
    elif out[0].dtype == F32:
        place = chunks[0] if spans == 1 else 0
        out_specs = [pl.BlockSpec((1, spans * width, v, v), lambda n, rows, *_: (rows[n], place, 0, 0))]
    else:
        out_specs = [
            pl.BlockSpec((width, 1, v, v), lambda n, *_, p=p: (0, jnp.clip(n - p * CAP, 0, CAP - 1), 0, 0))
            for p in range(len(out))
        ]
    added, added_specs = [], []
    if not flip:
        added = [*c, *[k] * spans]
        added_specs = [pl.BlockSpec(one_row, lambda n, rows, crows, *_: (crows[n], 0, 0, 0))] * spans
        added_specs += [pl.BlockSpec(one_row, lambda n, rows, *_, h=h: (rows[n], h, 0, 0)) for h in chunks]
    return pl.pallas_call(
        functools.partial(finish_kernel if into is None else kept_kernel, sets),
        out_shape=out,
        grid_spec=pltpu.PrefetchScalarGridSpec(
            num_scalar_prefetch=5,
            grid=(steps,),
            in_specs=[pl.BlockSpec(memory_space=pltpu.SMEM), resident(tall.shape), resident(wide.shape)]
            + [pl.BlockSpec(memory_space=pl.ANY)] * len(kept)
            + [resident(x.shape) for x in w]
            + added_specs
            + part,
            out_specs=out_specs,
            scratch_shapes=[
                pltpu.VMEM((v, v), F32),
                pltpu.VMEM((depth, v), BF16),
                pltpu.VMEM((width, v, v), BF16),
            ],
        ),
        input_output_aliases={} if into is None else {8: 0},
        compiler_params=params(),
        cost_estimate=cost(
            2 * steps * spans * width * v * v * depth, 2 * spans * width * v * (depth + steps * v * 5)
        ),
        name="finish",
    )(rows, crows, where, held, use, occ, tall, wide, *kept, *w, *added, *parts)


def joined_kernel(groups, rows_ref, where_ref, occ_ref, tall_ref, wide_ref, into_ref, *refs):
    ct_ref, k_ref, o_ref = refs[-3:]
    taken, width, v, _ = o_ref.shape
    w_refs, t_refs = refs[:taken], refs[taken : taken + groups]
    first = pl.program_id(0) * taken

    def column(j, carry):
        left = jnp.concatenate([w[0] for w in w_refs], axis=0)
        product = jnp.dot(left, stacked(t_refs, j), preferred_element_type=F32).astype(BF16)
        for q in range(taken):
            base = tall_ref[...] + wide_ref[...] - occ_ref[where_ref[0] + rows_ref[first + q]]
            total = k_ref[q, j].astype(F32) + product[q * v : (q + 1) * v].astype(F32) + ct_ref[q, j].astype(F32)
            o_ref[q, j] = total / (base - occ_ref[where_ref[1] + where_ref[3] + j])
        return carry

    lax.fori_loop(0, width, column, 0)


def joined(wp, parts, chunk, ct, k, tall, wide, occ, where, rows, into):
    width, _, v, _ = parts[0].shape
    depth, steps = wp.shape[2], rows.shape[0] // width
    where = jnp.concatenate([where, jnp.full((1,), chunk * width, I32)])
    block = (width, width, v, v)
    by_row = pl.BlockSpec(block, lambda n, rows, where: (rows[n * width] // width, chunk, 0, 0))
    return pl.pallas_call(
        functools.partial(joined_kernel, len(parts)),
        out_shape=jax.ShapeDtypeStruct(into.shape, into.dtype),
        grid_spec=pltpu.PrefetchScalarGridSpec(
            num_scalar_prefetch=2,
            grid=(steps,),
            in_specs=[pl.BlockSpec(memory_space=pltpu.SMEM), resident(tall.shape), resident(wide.shape)]
            + [pl.BlockSpec(memory_space=pl.ANY)]
            + [
                pl.BlockSpec((1, v, depth), lambda n, rows, where, q=q: (rows[n * width + q], 0, 0))
                for q in range(width)
            ]
            + [resident(p.shape) for p in parts]
            + [pl.BlockSpec(block, lambda n, rows, where: (n, 0, 0, 0)), by_row],
            out_specs=by_row,
        ),
        input_output_aliases={5: 0},
        compiler_params=params(),
        cost_estimate=cost(2 * steps * width**2 * v * v * depth, 2 * steps * width * v * (depth + 4 * width * v)),
        name="joined",
    )(rows, where, occ, tall, wide, into, *[wp] * width, *parts, ct, k)


class Links:
    def __init__(self, groups, jgroups):
        self.groups, self.jgroups, self.ratio = groups, jgroups, jgroups // groups

    def near(self, x, s):
        return lax.ppermute(x, "igrp", [(i, i ^ s) for i in range(self.groups)])

    def route(self, x, s):
        pairs = [
            (i * self.jgroups + z * self.ratio + y, z * self.jgroups + (i ^ s) * self.ratio + y)
            for i in range(self.groups)
            for z in range(self.groups)
            for y in range(self.ratio)
        ]
        return lax.ppermute(x, AXES, pairs)

    def swap(self, x, d):
        return lax.ppermute(x, "jgrp", [(j, j ^ d) for j in range(self.jgroups)])

    def spread(self, w, bit):
        held = [h for h in range(self.groups) if h % (2 * bit) == 0]
        pairs = [
            ((z ^ h) * self.jgroups + z * self.ratio + y, (z ^ h ^ bit) * self.jgroups + z * self.ratio + y)
            for h in held
            for z in range(self.groups)
            for y in range(self.ratio)
        ]
        return lax.ppermute(w, AXES, pairs)

    def bits(self):
        bit, found = self.groups // 2, []
        while bit:
            found.append(bit)
            bit //= 2
        return found


def exchange(links, mine, near, far, window, rider=None):
    groups, chunks = links.groups, range(len(near))
    sides = [list(range(p, groups, 2)) for p in range(2)]
    steps = [(h, side) for h in chunks for side in sides]
    plan = [[] for _ in range(len(steps) + 1)]
    for h in chunks:
        for s in range(1, groups):
            at = 2 * h + s % 2 if s > 1 else h * len(steps)
            plan[min(at, len(steps))].append((h, s))
    earlier, before = [], []
    for t in range(len(steps) + 1):
        slots = []
        if t < len(steps):
            h, side = steps[t]
            slots += [(mine[h], s) for s in side]
        if t > 0:
            back, back_side = steps[t - 1]
            slots += [(far[0][back], s) for s in back_side]
        for g, s in plan[t]:
            if not any(x is mine[g] and n == s for x, n in slots):
                slots.append((mine[g], s))
        arrays = [x[n] for x, n in slots]
        riding = rider is not None and t == len(steps)
        if riding:
            arrays.append(rider[0])
        if earlier:
            arrays = tie(arrays, earlier)
        for (x, n), array in zip(slots, arrays):
            x[n] = array
        earlier = []
        if t < len(steps):
            for s in side:
                far[0][h][s] = links.route(mine[h][s], s)
                earlier.append(far[0][h][s])
        if t > 0:
            for d in range(1, links.ratio):
                for s in back_side:
                    far[d][back][s] = links.swap(far[0][back][s], d)
                    earlier.append(far[d][back][s])
        for g, s in plan[t]:
            near[g][s] = links.near(mine[g][s], s)
            earlier.append(near[g][s])
        for g in chunks:
            near[g][0] = mine[g][0]
        earlier, before = earlier + window(t, before), earlier
        if riding:
            earlier.append(rider[1](arrays[-1]))
    return earlier


def body(t_start, integrals, weights, neighbours, eps_occ, eps_vir):
    row_count, cols, v, _ = t_start.shape
    groups, jgroups = lax.axis_size("igrp"), lax.axis_size("jgrp")
    links = Links(groups, jgroups)
    ratio = links.ratio
    my_i, my_j = lax.axis_index("igrp"), lax.axis_index("jgrp")
    my_z, my_half = my_j // ratio, my_j % ratio
    width = cols // 2
    chunks = range(2)
    sides = [list(range(p, groups, 2)) for p in range(2)]

    lists = listed_offsets(neighbours, groups, row_count)
    slots = relative_slots(neighbours, lists, groups, row_count)
    asked = lax.dynamic_slice_in_dim(lists, my_i, 1, 1)[:, 0]
    order = my_i ^ jnp.arange(groups, dtype=I32)
    rows = jnp.sum(
        asked[None] * (jnp.arange(groups, dtype=I32)[None, :, None] == order[:, None, None]).astype(I32), axis=1
    ).reshape(-1)
    every_row = jnp.arange(row_count, dtype=I32)
    where = jnp.stack([my_i * row_count, my_j * cols, my_half]).astype(I32)
    tall, wide = eps_vir.reshape(v, 1), eps_vir.reshape(1, v)

    def slots_of(first, count):
        return lax.dynamic_slice_in_dim(slots, first, count, 0)

    def empty():
        return [[None] * groups for _ in chunks], [[[None] * groups for _ in chunks] for _ in range(ratio)]

    made = {}

    def opening(t, earlier):
        if t == 0:
            made["wp"] = slotted([weights], jnp.zeros((), I32), slots_of(my_i * row_count, row_count), groups)
            return [made["wp"]]
        if t in (2, 4):
            made["c", t // 2 - 1] = direct(made["wp"], rows, near[t // 2 - 1])
            return [made["c", t // 2 - 1]]
        return []

    bits = links.bits()
    apart = my_i ^ my_z

    def fresh(bit):
        return apart % (2 * bit) == bit

    def deliver(h, w, came, bit, later):
        while later:
            w = jnp.where(fresh(bit), came, w)
            bit, later = later[0], later[1:]
            came = links.spread(w, bit)
        return slotted([w, came], fresh(bit), slots_of(my_j * cols + h * width, width), groups)

    own_w = [lax.dynamic_slice_in_dim(weights, my_half * cols + h * width, width, 0) for h in chunks]
    mine = [[*pick_rows(t_start, rows, groups, width, h)] for h in chunks]
    near, far = empty()
    last = exchange(links, mine, near, far, opening, (own_w[0], lambda w: links.spread(w, bits[0])))
    came, second = tie([last.pop(), own_w[1]], last)
    second_came = links.spread(second, bits[0])
    wpj = [deliver(0, own_w[0], came, bits[0], bits[1:]), None]

    def rows_of(h, halves):
        return jnp.concatenate(
            [(my_half ^ d) * cols + h * width + jnp.arange(width, dtype=I32) for d in halves]
        )

    chosen = ((rows // cols) ^ my_half) * len(chunks) + (rows % cols) // width
    in_order = jnp.arange(groups * CAP, dtype=I32)

    def listed_rows(h, c):
        return [
            *finish(
                wpj, [c], in_order, [h], integrals, tall, wide, eps_occ, where, rows, chosen,
                [piece for half in far_now for piece in half],
                [jax.ShapeDtypeStruct((width, CAP, v, v), BF16)] * groups,
            )
        ]

    for sweep in range(ITERS - 1):
        c = [made["c", h] if sweep == 0 else direct(made["wp"], rows, near[h]) for h in chunks]
        far_now = far
        mine = [listed_rows(0, c[0]), [None] * groups]
        near, far = empty()
        final = sweep == ITERS - 2
        state = {}
        every, first_half = range(ratio), jnp.zeros((width,), I32)

        def complete(over, h, halves):
            some_rows = rows_of(h, halves)
            use = jnp.repeat(jnp.arange(len(halves), dtype=I32), width)
            [state["out"]] = finish(
                wpj, [state["c", n] for n in over], some_rows, over, integrals, tall, wide, eps_occ, where, some_rows,
                use, [far[d][h] for d in halves], [jax.ShapeDtypeStruct((row_count, cols, v, v), F32)], state.get("out"),
            )
            return state["out"]

        def middle(t, earlier):
            if t == 1:
                if wpj[1] is None:
                    [arrived] = tie([second_came], earlier)
                    wpj[1] = deliver(1, second, arrived, bits[0], bits[1:])
                mine[1][:] = listed_rows(1, c[1])
                return mine[1]
            if t == 0 or not final:
                return []
            if t == 2:
                state["c", 0] = direct(made["wp"], every_row, near[0])
                return [state["c", 0]]
            if t == 3:
                some_rows = rows_of(0, every)
                use = jnp.repeat(jnp.arange(ratio, dtype=I32), width)
                [state["ct"]] = finish(
                    wpj, None, some_rows, [1], integrals, tall, wide, eps_occ, where, some_rows, use,
                    [far[d][0] for d in every],
                    [jax.ShapeDtypeStruct((ratio * width, width, v, v), BF16)],
                )
                return [state["ct"], complete([0], 0, every)]
            return []

        exchange(links, mine, near, far, middle)
    state["c", 1] = direct(made["wp"], rows_of(1, every), near[1], placed=True)
    complete([0, 1], 1, [0])
    state["out"] = joined(
        made["wp"], near[1], 1, state["ct"], integrals, tall, wide, eps_occ, where, rows_of(0, every), state["out"]
    )
    for d in every[1:]:
        complete([0, 1], 1, [d])
    return state["out"]


def solution(mesh):
    placed = (
        P("igrp", "jgrp", None, None),
        P("igrp", "jgrp", None, None),
        P("igrp", None, None, None),
        P(),
        P(),
        P(),
    )
    return jax.shard_map(
        body, mesh=mesh, in_specs=placed, out_specs=P("igrp", "jgrp", None, None), check_vma=False
    )
```

```python
import functools

import jax
import jax.numpy as jnp
from jax import lax
from jax.experimental import pallas as pl
from jax.experimental.pallas import tpu as pltpu
from jax.sharding import PartitionSpec as P

CAP = 2
ITERS = 2
AXES = ("igrp", "jgrp")
VMEM = 38 * 2**20
F32, BF16, I32 = jnp.float32, jnp.bfloat16, jnp.int32


def params():
    return pltpu.CompilerParams(vmem_limit_bytes=VMEM)


def cost(flops, moved):
    return pl.CostEstimate(flops=flops, bytes_accessed=moved, transcendentals=0)


def resident(shape):
    return pl.BlockSpec(shape, lambda *_: (0,) * len(shape), pipeline_mode=pl.Buffered(1))


def listed_offsets(neighbours, groups, rows):
    named = neighbours.reshape(groups, -1)
    every = jnp.arange(groups * rows, dtype=I32)
    flags = jnp.any(named[:, :, None] == every[None, None, :], axis=1).reshape(groups, groups, rows)
    offsets = jnp.arange(rows, dtype=I32)
    before = (offsets[:, None] < offsets[None, :]).astype(I32)
    rank = jnp.sum(flags.astype(I32)[:, :, :, None] * before[None, None], axis=2)
    hits = flags[:, :, :, None] & (rank[:, :, :, None] == jnp.arange(CAP, dtype=I32))
    return jnp.sum(hits.astype(I32) * offsets[None, None, :, None], axis=2)


def relative_slots(neighbours, lists, groups, rows):
    group = jnp.arange(groups, dtype=I32)[:, None, None]
    block = jnp.arange(groups, dtype=I32)[None, :, None]
    orbital = block * rows + lists
    slot = (group ^ block) * CAP + jnp.arange(CAP, dtype=I32)[None, None, :]
    grouped = neighbours.reshape(groups, -1)
    hits = (grouped[:, :, None, None] == orbital[:, None]).astype(I32)
    return jnp.sum(hits * slot[:, None], axis=(2, 3)).reshape(neighbours.shape)


def pick_kernel(rows_ref, *refs):
    half = len(refs) // 2
    for source, target in zip(refs[:half], refs[half:]):
        target[:, 0] = source[0]


def pick_rows(t, rows, groups, width, chunk):
    v = t.shape[-1]
    return pl.pallas_call(
        pick_kernel,
        out_shape=[jax.ShapeDtypeStruct((width, CAP, v, v), t.dtype)] * groups,
        grid_spec=pltpu.PrefetchScalarGridSpec(
            num_scalar_prefetch=1,
            grid=(CAP,),
            in_specs=[
                pl.BlockSpec((1, width, v, v), lambda c, rows, s=s: (rows[s * CAP + c], chunk, 0, 0))
                for s in range(groups)
            ],
            out_specs=[pl.BlockSpec((width, 1, v, v), lambda c, rows: (0, c, 0, 0))] * groups,
        ),
        compiler_params=params(),
        cost_estimate=cost(0, 4 * groups * CAP * width * v * v),
        name="pick_rows",
    )(rows, *[t] * groups)


def tie_kernel(*refs):
    pass


def tie(arrays, earlier):
    if not arrays:
        return arrays
    known = {id(x) for x in arrays}
    earlier = [x for x in earlier if id(x) not in known]
    return pl.pallas_call(
        tie_kernel,
        out_shape=[jax.ShapeDtypeStruct(x.shape, x.dtype) for x in arrays],
        in_specs=[pl.BlockSpec(memory_space=pl.ANY)] * (len(arrays) + len(earlier)),
        out_specs=[pl.BlockSpec(memory_space=pl.ANY)] * len(arrays),
        input_output_aliases={n: n for n in range(len(arrays))},
        name="tie",
    )(*arrays, *earlier)


def slotted_kernel(slots_ref, pick_ref, *refs):
    w_refs, o_ref = refs[:-1], refs[-1]
    listed, v = w_refs[0].shape[1], w_refs[0].shape[2]
    row = pl.program_id(0) * listed
    if o_ref.shape[2] > listed * v:
        o_ref[...] = jnp.zeros_like(o_ref)

    def place(w_ref):
        for m in range(listed):
            start = pl.multiple_of(slots_ref[row + m] * v, v)
            o_ref[0, :, pl.ds(start, v)] = w_ref[0, m]

    for n, w_ref in enumerate(w_refs):
        pl.when(pick_ref[0] == n)(functools.partial(place, w_ref))


def slotted(sources, pick, slots, groups):
    rows, listed, v, _ = sources[0].shape
    depth = groups * CAP * v
    return pl.pallas_call(
        slotted_kernel,
        out_shape=jax.ShapeDtypeStruct((rows, v, depth), sources[0].dtype),
        grid_spec=pltpu.PrefetchScalarGridSpec(
            num_scalar_prefetch=2,
            grid=(rows,),
            in_specs=[
                pl.BlockSpec((1, listed, v, v), lambda i, slots, pick, n=n: (jnp.where(pick[0] == n, i, 0), 0, 0, 0))
                for n in range(len(sources))
            ],
            out_specs=pl.BlockSpec((1, v, depth), lambda i, slots, pick: (i, 0, 0)),
        ),
        compiler_params=params(),
        cost_estimate=cost(0, 4 * rows * v * depth),
        name="slotted",
    )(slots.reshape(-1), jnp.reshape(pick, (1,)).astype(I32), *sources)


def stacked(refs, at):
    v = refs[0].shape[-1]
    return jnp.concatenate([r[at].reshape(-1, v) for r in refs], axis=0)


def direct_kernel(taken, rows_ref, *refs):
    w_refs, t_refs, o_ref = refs[:taken], refs[taken:-1], refs[-1]
    cols, v = o_ref.shape[1], o_ref.shape[2]

    def column(j, carry):
        left = jnp.concatenate([w[0] for w in w_refs], axis=0)
        product = jnp.dot(left, stacked(t_refs, j), preferred_element_type=F32).astype(BF16)
        for q in range(taken):
            o_ref[q, j] = product[q * v : (q + 1) * v]
        return carry

    lax.fori_loop(0, cols, column, 0)


def direct(wp, rows, parts, placed=False):
    cols, _, v, _ = parts[0].shape
    count, depth = rows.shape[0], wp.shape[2]
    taken = cols if placed else 4 if count % 4 == 0 else 1
    return pl.pallas_call(
        functools.partial(direct_kernel, taken),
        out_shape=jax.ShapeDtypeStruct((wp.shape[0] if placed else count, cols, v, v), BF16),
        grid_spec=pltpu.PrefetchScalarGridSpec(
            num_scalar_prefetch=1,
            grid=(count // taken,),
            in_specs=[
                pl.BlockSpec((1, v, depth), lambda n, rows, q=q: (rows[n * taken + q], 0, 0))
                for q in range(taken)
            ]
            + [resident(p.shape) for p in parts],
            out_specs=pl.BlockSpec(
                (taken, cols, v, v), lambda n, rows: (rows[n * taken] // taken if placed else n, 0, 0, 0)
            ),
        ),
        compiler_params=params(),
        cost_estimate=cost(2 * count * cols * v * v * depth, 2 * count * v * (depth + cols * v)),
        name="direct",
    )(rows, *[wp] * taken, *parts)


def finish_kernel(sets, rows_ref, crows_ref, where_ref, held_ref, use_ref, occ_ref, tall_ref, wide_ref, *refs):
    (spans, groups), choices, outs, flip = sets
    base_ref, right_ref, made_ref = refs[-3:]
    o_refs = refs[-3 - outs : -3]
    w_refs, refs = refs[:spans], refs[spans:]
    if not flip:
        c_refs, k_refs, refs = refs[:spans], refs[spans : 2 * spans], refs[2 * spans :]
    t_refs = refs[: choices * groups]
    width, v, depth = w_refs[0].shape
    step = pl.program_id(0)
    if not flip:
        base_ref[...] = tall_ref[...] + wide_ref[...] - occ_ref[where_ref[0] + rows_ref[step]]

    def load(first):
        for s in range(groups):
            piece = t_refs[first * groups + s][0].reshape(CAP * v, v)
            right_ref[s * CAP * v : (s + 1) * CAP * v] = piece

    if choices > 1:
        for n in range(choices):
            pl.when(use_ref[step] == n)(functools.partial(load, n))
    for n in range(spans):
        left = w_refs[n][...].reshape(width * v, depth)
        right = right_ref[...] if choices > 1 else stacked(t_refs, 0)
        product = jnp.dot(left, right, preferred_element_type=F32).astype(BF16)
        for j in range(width):
            value = product[j * v : (j + 1) * v].astype(F32).T
            if not flip:
                total = k_refs[n][0, j].astype(F32) + c_refs[n][0, j].astype(F32) + value
                column = where_ref[1] + where_ref[3] + n * width + j
                value = total / (base_ref[...] - occ_ref[column])
            value = value.astype(o_refs[0].dtype)
            if outs > 1:
                made_ref[j] = value
            else:
                o_refs[0][0, n * width + j] = value

    def store(o_ref):
        o_ref[:, 0] = made_ref[...]

    if outs > 1:
        for p in range(outs):
            pl.when(step // CAP == p)(functools.partial(store, o_refs[p]))


def kept_kernel(sets, *refs):
    finish_kernel(sets, *refs[:8], *refs[9:])


def finish(w, c, crows, chunks, k, tall, wide, occ, where, rows, use, far, out, into=None):
    w = [w[h] for h in chunks]
    width, v, depth = w[0].shape
    choices, groups = len(far), len(far[0])
    parts = [t for one in far for t in one]
    spans, steps = len(chunks), rows.shape[0]
    flip = c is None
    where = jnp.concatenate([where, jnp.full((1,), chunks[0] * width, I32)])
    at = rows % width
    reads = use[None] == jnp.arange(choices, dtype=I32)[:, None]
    order = jnp.arange(steps, dtype=I32)
    gap = order[None] - order[:, None]
    rank = jnp.where(gap >= 0, gap, steps - gap)
    rank = jnp.where(reads[:, None], rank[None], 4 * steps)
    nearest = (rank == jnp.min(rank, axis=2, keepdims=True)).astype(I32)
    held = jnp.where(jnp.any(reads, axis=1)[:, None], jnp.sum(nearest * at, axis=2), 0).reshape(-1)
    part = [
        pl.BlockSpec((1, CAP, v, v), lambda n, rows, crows, where, held, use, i=i: (held[i * steps + n], 0, 0, 0))
        for i in range(choices)
        for _ in range(groups)
    ]
    one_row = (1, width, v, v)
    kept = [] if into is None else [into]
    sets = ((spans, groups), choices, len(out), flip)
    if flip:
        out_specs = [pl.BlockSpec(one_row, lambda n, *_: (n, 0, 0, 0))]
    elif out[0].dtype == F32:
        place = chunks[0] if spans == 1 else 0
        out_specs = [pl.BlockSpec((1, spans * width, v, v), lambda n, rows, *_: (rows[n], place, 0, 0))]
    else:
        out_specs = [
            pl.BlockSpec((width, 1, v, v), lambda n, *_, p=p: (0, jnp.clip(n - p * CAP, 0, CAP - 1), 0, 0))
            for p in range(len(out))
        ]
    added, added_specs = [], []
    if not flip:
        added = [*c, *[k] * spans]
        added_specs = [pl.BlockSpec(one_row, lambda n, rows, crows, *_: (crows[n], 0, 0, 0))] * spans
        added_specs += [pl.BlockSpec(one_row, lambda n, rows, *_, h=h: (rows[n], h, 0, 0)) for h in chunks]
    return pl.pallas_call(
        functools.partial(finish_kernel if into is None else kept_kernel, sets),
        out_shape=out,
        grid_spec=pltpu.PrefetchScalarGridSpec(
            num_scalar_prefetch=5,
            grid=(steps,),
            in_specs=[pl.BlockSpec(memory_space=pltpu.SMEM), resident(tall.shape), resident(wide.shape)]
            + [pl.BlockSpec(memory_space=pl.ANY)] * len(kept)
            + [resident(x.shape) for x in w]
            + added_specs
            + part,
            out_specs=out_specs,
            scratch_shapes=[
                pltpu.VMEM((v, v), F32),
                pltpu.VMEM((depth, v), BF16),
                pltpu.VMEM((width, v, v), BF16),
            ],
        ),
        input_output_aliases={} if into is None else {8: 0},
        compiler_params=params(),
        cost_estimate=cost(
            2 * steps * spans * width * v * v * depth, 2 * spans * width * v * (depth + steps * v * 5)
        ),
        name="finish",
    )(rows, crows, where, held, use, occ, tall, wide, *kept, *w, *added, *parts)


def joined_kernel(groups, rows_ref, where_ref, occ_ref, tall_ref, wide_ref, into_ref, *refs):
    ct_ref, k_ref, o_ref = refs[-3:]
    taken, width, v, _ = o_ref.shape
    w_refs, t_refs = refs[:taken], refs[taken : taken + groups]
    first = pl.program_id(0) * taken

    def column(j, carry):
        left = jnp.concatenate([w[0] for w in w_refs], axis=0)
        product = jnp.dot(left, stacked(t_refs, j), preferred_element_type=F32).astype(BF16)
        for q in range(taken):
            base = tall_ref[...] + wide_ref[...] - occ_ref[where_ref[0] + rows_ref[first + q]]
            total = k_ref[q, j].astype(F32) + product[q * v : (q + 1) * v].astype(F32) + ct_ref[q, j].astype(F32)
            o_ref[q, j] = total / (base - occ_ref[where_ref[1] + where_ref[3] + j])
        return carry

    lax.fori_loop(0, width, column, 0)


def joined(wp, parts, chunk, ct, k, tall, wide, occ, where, rows, into):
    width, _, v, _ = parts[0].shape
    depth, steps = wp.shape[2], rows.shape[0] // width
    where = jnp.concatenate([where, jnp.full((1,), chunk * width, I32)])
    block = (width, width, v, v)
    by_row = pl.BlockSpec(block, lambda n, rows, where: (rows[n * width] // width, chunk, 0, 0))
    return pl.pallas_call(
        functools.partial(joined_kernel, len(parts)),
        out_shape=jax.ShapeDtypeStruct(into.shape, into.dtype),
        grid_spec=pltpu.PrefetchScalarGridSpec(
            num_scalar_prefetch=2,
            grid=(steps,),
            in_specs=[pl.BlockSpec(memory_space=pltpu.SMEM), resident(tall.shape), resident(wide.shape)]
            + [pl.BlockSpec(memory_space=pl.ANY)]
            + [
                pl.BlockSpec((1, v, depth), lambda n, rows, where, q=q: (rows[n * width + q], 0, 0))
                for q in range(width)
            ]
            + [resident(p.shape) for p in parts]
            + [pl.BlockSpec(block, lambda n, rows, where: (n, 0, 0, 0)), by_row],
            out_specs=by_row,
        ),
        input_output_aliases={5: 0},
        compiler_params=params(),
        cost_estimate=cost(2 * steps * width**2 * v * v * depth, 2 * steps * width * v * (depth + 4 * width * v)),
        name="joined",
    )(rows, where, occ, tall, wide, into, *[wp] * width, *parts, ct, k)


class Links:
    def __init__(self, groups, jgroups):
        self.groups, self.jgroups, self.ratio = groups, jgroups, jgroups // groups

    def near(self, x, s):
        return lax.ppermute(x, "igrp", [(i, i ^ s) for i in range(self.groups)])

    def route(self, x, s):
        pairs = [
            (i * self.jgroups + z * self.ratio + y, z * self.jgroups + (i ^ s) * self.ratio + y)
            for i in range(self.groups)
            for z in range(self.groups)
            for y in range(self.ratio)
        ]
        return lax.ppermute(x, AXES, pairs)

    def swap(self, x, d):
        return lax.ppermute(x, "jgrp", [(j, j ^ d) for j in range(self.jgroups)])

    def spread(self, w, held, bit):
        pairs = [
            ((z ^ held) * self.jgroups + z * self.ratio + y, (z ^ held ^ bit) * self.jgroups + z * self.ratio + y)
            for z in range(self.groups)
            for y in range(self.ratio)
        ]
        return lax.ppermute(w, AXES, pairs)

    def bits(self):
        bit, found = self.groups // 2, []
        while bit:
            found.append(bit)
            bit //= 2
        return found


def exchange(links, mine, near, far, window, rider=None):
    groups, chunks = links.groups, range(len(near))
    sides = [list(range(p, groups, 2)) for p in range(2)]
    steps = [(h, side) for h in chunks for side in sides]
    plan = [[] for _ in range(len(steps) + 1)]
    for h in chunks:
        for s in range(1, groups):
            at = 2 * h + s % 2 if s > 1 else h * len(steps)
            plan[min(at, len(steps))].append((h, s))
    earlier, before = [], []
    for t in range(len(steps) + 1):
        slots = []
        if t < len(steps):
            h, side = steps[t]
            slots += [(mine[h], s) for s in side]
        if t > 0:
            back, back_side = steps[t - 1]
            slots += [(far[0][back], s) for s in back_side]
        for g, s in plan[t]:
            if not any(x is mine[g] and n == s for x, n in slots):
                slots.append((mine[g], s))
        arrays = [x[n] for x, n in slots]
        riding = rider is not None and t == len(steps)
        if riding:
            arrays.append(rider[0])
        if earlier:
            arrays = tie(arrays, earlier)
        for (x, n), array in zip(slots, arrays):
            x[n] = array
        earlier = []
        if t < len(steps):
            for s in side:
                far[0][h][s] = links.route(mine[h][s], s)
                earlier.append(far[0][h][s])
        if t > 0:
            for d in range(1, links.ratio):
                for s in back_side:
                    far[d][back][s] = links.swap(far[0][back][s], d)
                    earlier.append(far[d][back][s])
        for g, s in plan[t]:
            near[g][s] = links.near(mine[g][s], s)
            earlier.append(near[g][s])
        for g in chunks:
            near[g][0] = mine[g][0]
        earlier, before = earlier + window(t, before), earlier
        if riding:
            earlier.append(rider[1](arrays[-1]))
    return earlier


def body(t_start, integrals, weights, neighbours, eps_occ, eps_vir):
    row_count, cols, v, _ = t_start.shape
    groups, jgroups = lax.axis_size("igrp"), lax.axis_size("jgrp")
    links = Links(groups, jgroups)
    ratio = links.ratio
    my_i, my_j = lax.axis_index("igrp"), lax.axis_index("jgrp")
    my_z, my_half = my_j // ratio, my_j % ratio
    width = cols // 2
    chunks = range(2)
    sides = [list(range(p, groups, 2)) for p in range(2)]

    lists = listed_offsets(neighbours, groups, row_count)
    slots = relative_slots(neighbours, lists, groups, row_count)
    asked = lax.dynamic_slice_in_dim(lists, my_i, 1, 1)[:, 0]
    order = my_i ^ jnp.arange(groups, dtype=I32)
    rows = jnp.sum(
        asked[None] * (jnp.arange(groups, dtype=I32)[None, :, None] == order[:, None, None]).astype(I32), axis=1
    ).reshape(-1)
    every_row = jnp.arange(row_count, dtype=I32)
    where = jnp.stack([my_i * row_count, my_j * cols, my_half]).astype(I32)
    tall, wide = eps_vir.reshape(v, 1), eps_vir.reshape(1, v)

    def slots_of(first, count):
        return lax.dynamic_slice_in_dim(slots, first, count, 0)

    def empty():
        return [[None] * groups for _ in chunks], [[[None] * groups for _ in chunks] for _ in range(ratio)]

    made = {}

    def opening(t, earlier):
        if t == 0:
            made["wp"] = slotted([weights], jnp.zeros((), I32), slots_of(my_i * row_count, row_count), groups)
            return [made["wp"]]
        if t in (2, 4):
            made["c", t // 2 - 1] = direct(made["wp"], rows, near[t // 2 - 1])
            return [made["c", t // 2 - 1]]
        return []

    bits = links.bits()

    def deliver(h, w, far_side):
        there = {0: w, bits[0]: far_side}
        for bit in bits[1:]:
            for held in list(there):
                there[held ^ bit] = links.spread(there[held], held, bit)
        sources = [there[n] for n in range(groups)]
        return slotted(sources, my_i ^ my_z, slots_of(my_j * cols + h * width, width), groups)

    own_w = [lax.dynamic_slice_in_dim(weights, my_half * cols + h * width, width, 0) for h in chunks]
    mine = [[*pick_rows(t_start, rows, groups, width, h)] for h in chunks]
    near, far = empty()
    last = exchange(links, mine, near, far, opening, (own_w[0], lambda w: links.spread(w, 0, bits[0])))
    came, second = tie([last.pop(), own_w[1]], last)
    second_came = links.spread(second, 0, bits[0])
    wpj = [deliver(0, own_w[0], came), None]

    def rows_of(h, halves):
        return jnp.concatenate(
            [(my_half ^ d) * cols + h * width + jnp.arange(width, dtype=I32) for d in halves]
        )

    chosen = ((rows // cols) ^ my_half) * len(chunks) + (rows % cols) // width
    in_order = jnp.arange(groups * CAP, dtype=I32)

    def listed_rows(h, c):
        return [
            *finish(
                wpj, [c], in_order, [h], integrals, tall, wide, eps_occ, where, rows, chosen,
                [piece for half in far_now for piece in half],
                [jax.ShapeDtypeStruct((width, CAP, v, v), BF16)] * groups,
            )
        ]

    for sweep in range(ITERS - 1):
        c = [made["c", h] if sweep == 0 else direct(made["wp"], rows, near[h]) for h in chunks]
        far_now = far
        mine = [listed_rows(0, c[0]), [None] * groups]
        near, far = empty()
        final = sweep == ITERS - 2
        state = {}
        every, first_half = range(ratio), jnp.zeros((width,), I32)

        def complete(over, h, halves):
            some_rows = rows_of(h, halves)
            use = jnp.repeat(jnp.arange(len(halves), dtype=I32), width)
            [state["out"]] = finish(
                wpj, [state["c", n] for n in over], some_rows, over, integrals, tall, wide, eps_occ, where, some_rows,
                use, [far[d][h] for d in halves], [jax.ShapeDtypeStruct((row_count, cols, v, v), F32)], state.get("out"),
            )
            return state["out"]

        def middle(t, earlier):
            if t == 1:
                if wpj[1] is None:
                    [arrived] = tie([second_came], earlier)
                    wpj[1] = deliver(1, second, arrived)
                mine[1][:] = listed_rows(1, c[1])
                return mine[1]
            if t == 0 or not final:
                return []
            if t == 2:
                state["c", 0] = direct(made["wp"], every_row, near[0])
                return [state["c", 0]]
            if t == 3:
                some_rows = rows_of(0, every)
                use = jnp.repeat(jnp.arange(ratio, dtype=I32), width)
                [state["ct"]] = finish(
                    wpj, None, some_rows, [1], integrals, tall, wide, eps_occ, where, some_rows, use,
                    [far[d][0] for d in every],
                    [jax.ShapeDtypeStruct((ratio * width, width, v, v), BF16)],
                )
                return [state["ct"], complete([0], 0, every)]
            return []

        exchange(links, mine, near, far, middle)
    state["c", 1] = direct(made["wp"], rows_of(1, every), near[1], placed=True)
    complete([0, 1], 1, [0])
    state["out"] = joined(
        made["wp"], near[1], 1, state["ct"], integrals, tall, wide, eps_occ, where, rows_of(0, every), state["out"]
    )
    for d in every[1:]:
        complete([0, 1], 1, [d])
    return state["out"]


def solution(mesh):
    placed = (
        P("igrp", "jgrp", None, None),
        P("igrp", "jgrp", None, None),
        P("igrp", None, None, None),
        P(),
        P(),
        P(),
    )
    return jax.shard_map(
        body, mesh=mesh, in_specs=placed, out_specs=P("igrp", "jgrp", None, None), check_vma=False
    )
```

```python
import functools

import jax
import jax.numpy as jnp
from jax import lax
from jax.experimental import pallas as pl
from jax.experimental.pallas import tpu as pltpu
from jax.sharding import PartitionSpec as P

CAP = 2
ITERS = 2
AXES = ("igrp", "jgrp")
VMEM = 38 * 2**20
F32, BF16, I32 = jnp.float32, jnp.bfloat16, jnp.int32


def params():
    return pltpu.CompilerParams(vmem_limit_bytes=VMEM)


def cost(flops, moved):
    return pl.CostEstimate(flops=flops, bytes_accessed=moved, transcendentals=0)


def resident(shape):
    return pl.BlockSpec(shape, lambda *_: (0,) * len(shape), pipeline_mode=pl.Buffered(1))


def listed_offsets(neighbours, groups, rows):
    named = neighbours.reshape(groups, -1)
    every = jnp.arange(groups * rows, dtype=I32)
    flags = jnp.any(named[:, :, None] == every[None, None, :], axis=1).reshape(groups, groups, rows)
    offsets = jnp.arange(rows, dtype=I32)
    before = (offsets[:, None] < offsets[None, :]).astype(I32)
    rank = jnp.sum(flags.astype(I32)[:, :, :, None] * before[None, None], axis=2)
    hits = flags[:, :, :, None] & (rank[:, :, :, None] == jnp.arange(CAP, dtype=I32))
    return jnp.sum(hits.astype(I32) * offsets[None, None, :, None], axis=2)


def relative_slots(neighbours, lists, groups, rows):
    group = jnp.arange(groups, dtype=I32)[:, None, None]
    block = jnp.arange(groups, dtype=I32)[None, :, None]
    orbital = block * rows + lists
    slot = (group ^ block) * CAP + jnp.arange(CAP, dtype=I32)[None, None, :]
    grouped = neighbours.reshape(groups, -1)
    hits = (grouped[:, :, None, None] == orbital[:, None]).astype(I32)
    return jnp.sum(hits * slot[:, None], axis=(2, 3)).reshape(neighbours.shape)


def pick_kernel(rows_ref, *refs):
    half = len(refs) // 2
    for source, target in zip(refs[:half], refs[half:]):
        target[:, 0] = source[0]


def pick_rows(t, rows, groups, width, chunk):
    v = t.shape[-1]
    return pl.pallas_call(
        pick_kernel,
        out_shape=[jax.ShapeDtypeStruct((width, CAP, v, v), t.dtype)] * groups,
        grid_spec=pltpu.PrefetchScalarGridSpec(
            num_scalar_prefetch=1,
            grid=(CAP,),
            in_specs=[
                pl.BlockSpec((1, width, v, v), lambda c, rows, s=s: (rows[s * CAP + c], chunk, 0, 0))
                for s in range(groups)
            ],
            out_specs=[pl.BlockSpec((width, 1, v, v), lambda c, rows: (0, c, 0, 0))] * groups,
        ),
        compiler_params=params(),
        cost_estimate=cost(0, 4 * groups * CAP * width * v * v),
        name="pick_rows",
    )(rows, *[t] * groups)


def tie_kernel(*refs):
    pass


def tie(arrays, earlier):
    if not arrays:
        return arrays
    known = {id(x) for x in arrays}
    earlier = [x for x in earlier if id(x) not in known]
    return pl.pallas_call(
        tie_kernel,
        out_shape=[jax.ShapeDtypeStruct(x.shape, x.dtype) for x in arrays],
        in_specs=[pl.BlockSpec(memory_space=pl.ANY)] * (len(arrays) + len(earlier)),
        out_specs=[pl.BlockSpec(memory_space=pl.ANY)] * len(arrays),
        input_output_aliases={n: n for n in range(len(arrays))},
        name="tie",
    )(*arrays, *earlier)


def slotted_kernel(slots_ref, pick_ref, *refs):
    w_refs, o_ref = refs[:-1], refs[-1]
    listed, v = w_refs[0].shape[1], w_refs[0].shape[2]
    row = pl.program_id(0) * listed
    if o_ref.shape[2] > listed * v:
        o_ref[...] = jnp.zeros_like(o_ref)

    def place(w_ref):
        for m in range(listed):
            start = pl.multiple_of(slots_ref[row + m] * v, v)
            o_ref[0, :, pl.ds(start, v)] = w_ref[0, m]

    for n, w_ref in enumerate(w_refs):
        pl.when(pick_ref[0] == n)(functools.partial(place, w_ref))


def slotted(sources, pick, slots, groups):
    rows, listed, v, _ = sources[0].shape
    depth = groups * CAP * v
    return pl.pallas_call(
        slotted_kernel,
        out_shape=jax.ShapeDtypeStruct((rows, v, depth), sources[0].dtype),
        grid_spec=pltpu.PrefetchScalarGridSpec(
            num_scalar_prefetch=2,
            grid=(rows,),
            in_specs=[
                pl.BlockSpec((1, listed, v, v), lambda i, slots, pick, n=n: (jnp.where(pick[0] == n, i, 0), 0, 0, 0))
                for n in range(len(sources))
            ],
            out_specs=pl.BlockSpec((1, v, depth), lambda i, slots, pick: (i, 0, 0)),
        ),
        compiler_params=params(),
        cost_estimate=cost(0, 4 * rows * v * depth),
        name="slotted",
    )(slots.reshape(-1), jnp.reshape(pick, (1,)).astype(I32), *sources)


def stacked(refs, at):
    v = refs[0].shape[-1]
    return jnp.concatenate([r[at].reshape(-1, v) for r in refs], axis=0)


def direct_kernel(taken, rows_ref, *refs):
    w_refs, t_refs, o_ref = refs[:taken], refs[taken:-1], refs[-1]
    cols, v = o_ref.shape[1], o_ref.shape[2]

    def column(j, carry):
        left = jnp.concatenate([w[0] for w in w_refs], axis=0)
        product = jnp.dot(left, stacked(t_refs, j), preferred_element_type=F32).astype(BF16)
        for q in range(taken):
            o_ref[q, j] = product[q * v : (q + 1) * v]
        return carry

    lax.fori_loop(0, cols, column, 0)


def direct(wp, rows, parts, placed=False):
    cols, _, v, _ = parts[0].shape
    count, depth = rows.shape[0], wp.shape[2]
    taken = cols if placed else 4 if count % 4 == 0 else 1
    return pl.pallas_call(
        functools.partial(direct_kernel, taken),
        out_shape=jax.ShapeDtypeStruct((wp.shape[0] if placed else count, cols, v, v), BF16),
        grid_spec=pltpu.PrefetchScalarGridSpec(
            num_scalar_prefetch=1,
            grid=(count // taken,),
            in_specs=[
                pl.BlockSpec((1, v, depth), lambda n, rows, q=q: (rows[n * taken + q], 0, 0))
                for q in range(taken)
            ]
            + [resident(p.shape) for p in parts],
            out_specs=pl.BlockSpec(
                (taken, cols, v, v), lambda n, rows: (rows[n * taken] // taken if placed else n, 0, 0, 0)
            ),
        ),
        compiler_params=params(),
        cost_estimate=cost(2 * count * cols * v * v * depth, 2 * count * v * (depth + cols * v)),
        name="direct",
    )(rows, *[wp] * taken, *parts)


def finish_kernel(sets, rows_ref, crows_ref, where_ref, held_ref, use_ref, occ_ref, tall_ref, wide_ref, *refs):
    (spans, groups), choices, outs, flip = sets
    base_ref, right_ref, made_ref = refs[-3:]
    o_refs = refs[-3 - outs : -3]
    w_refs, refs = refs[:spans], refs[spans:]
    if not flip:
        c_refs, k_refs, refs = refs[:spans], refs[spans : 2 * spans], refs[2 * spans :]
    t_refs = refs[: choices * groups]
    width, v, depth = w_refs[0].shape
    step = pl.program_id(0)
    if not flip:
        base_ref[...] = tall_ref[...] + wide_ref[...] - occ_ref[where_ref[0] + rows_ref[step]]

    def load(first):
        for s in range(groups):
            piece = t_refs[first * groups + s][0].reshape(CAP * v, v)
            right_ref[s * CAP * v : (s + 1) * CAP * v] = piece

    if choices > 1:
        for n in range(choices):
            pl.when(use_ref[step] == n)(functools.partial(load, n))
    for n in range(spans):
        left = w_refs[n][...].reshape(width * v, depth)
        right = right_ref[...] if choices > 1 else stacked(t_refs, 0)
        product = jnp.dot(left, right, preferred_element_type=F32).astype(BF16)
        for j in range(width):
            value = product[j * v : (j + 1) * v].astype(F32).T
            if not flip:
                total = k_refs[n][0, j].astype(F32) + c_refs[n][0, j].astype(F32) + value
                column = where_ref[1] + where_ref[3] + n * width + j
                value = total / (base_ref[...] - occ_ref[column])
            value = value.astype(o_refs[0].dtype)
            if outs > 1:
                made_ref[j] = value
            else:
                o_refs[0][0, n * width + j] = value

    def store(o_ref):
        o_ref[:, 0] = made_ref[...]

    if outs > 1:
        for p in range(outs):
            pl.when(step // CAP == p)(functools.partial(store, o_refs[p]))


def kept_kernel(sets, *refs):
    finish_kernel(sets, *refs[:8], *refs[9:])


def finish(w, c, crows, chunks, k, tall, wide, occ, where, rows, use, far, out, into=None):
    w = [w[h] for h in chunks]
    width, v, depth = w[0].shape
    choices, groups = len(far), len(far[0])
    parts = [t for one in far for t in one]
    spans, steps = len(chunks), rows.shape[0]
    flip = c is None
    where = jnp.concatenate([where, jnp.full((1,), chunks[0] * width, I32)])
    at = rows % width
    reads = use[None] == jnp.arange(choices, dtype=I32)[:, None]
    order = jnp.arange(steps, dtype=I32)
    gap = order[None] - order[:, None]
    rank = jnp.where(gap >= 0, gap, steps - gap)
    rank = jnp.where(reads[:, None], rank[None], 4 * steps)
    nearest = (rank == jnp.min(rank, axis=2, keepdims=True)).astype(I32)
    held = jnp.where(jnp.any(reads, axis=1)[:, None], jnp.sum(nearest * at, axis=2), 0).reshape(-1)
    part = [
        pl.BlockSpec((1, CAP, v, v), lambda n, rows, crows, where, held, use, i=i: (held[i * steps + n], 0, 0, 0))
        for i in range(choices)
        for _ in range(groups)
    ]
    one_row = (1, width, v, v)
    kept = [] if into is None else [into]
    sets = ((spans, groups), choices, len(out), flip)
    if flip:
        out_specs = [pl.BlockSpec(one_row, lambda n, *_: (n, 0, 0, 0))]
    elif out[0].dtype == F32:
        place = chunks[0] if spans == 1 else 0
        out_specs = [pl.BlockSpec((1, spans * width, v, v), lambda n, rows, *_: (rows[n], place, 0, 0))]
    else:
        out_specs = [
            pl.BlockSpec((width, 1, v, v), lambda n, *_, p=p: (0, jnp.clip(n - p * CAP, 0, CAP - 1), 0, 0))
            for p in range(len(out))
        ]
    added, added_specs = [], []
    if not flip:
        added = [*c, *[k] * spans]
        added_specs = [pl.BlockSpec(one_row, lambda n, rows, crows, *_: (crows[n], 0, 0, 0))] * spans
        added_specs += [pl.BlockSpec(one_row, lambda n, rows, *_, h=h: (rows[n], h, 0, 0)) for h in chunks]
    return pl.pallas_call(
        functools.partial(finish_kernel if into is None else kept_kernel, sets),
        out_shape=out,
        grid_spec=pltpu.PrefetchScalarGridSpec(
            num_scalar_prefetch=5,
            grid=(steps,),
            in_specs=[pl.BlockSpec(memory_space=pltpu.SMEM), resident(tall.shape), resident(wide.shape)]
            + [pl.BlockSpec(memory_space=pl.ANY)] * len(kept)
            + [resident(x.shape) for x in w]
            + added_specs
            + part,
            out_specs=out_specs,
            scratch_shapes=[
                pltpu.VMEM((v, v), F32),
                pltpu.VMEM((depth, v), BF16),
                pltpu.VMEM((width, v, v), BF16),
            ],
        ),
        input_output_aliases={} if into is None else {8: 0},
        compiler_params=params(),
        cost_estimate=cost(
            2 * steps * spans * width * v * v * depth, 2 * spans * width * v * (depth + steps * v * 5)
        ),
        name="finish",
    )(rows, crows, where, held, use, occ, tall, wide, *kept, *w, *added, *parts)


def joined_kernel(groups, rows_ref, where_ref, occ_ref, tall_ref, wide_ref, into_ref, *refs):
    ct_ref, k_ref, o_ref = refs[-3:]
    taken, width, v, _ = o_ref.shape
    w_refs, t_refs = refs[:taken], refs[taken : taken + groups]
    first = pl.program_id(0) * taken

    def column(j, carry):
        left = jnp.concatenate([w[0] for w in w_refs], axis=0)
        product = jnp.dot(left, stacked(t_refs, j), preferred_element_type=F32).astype(BF16)
        for q in range(taken):
            base = tall_ref[...] + wide_ref[...] - occ_ref[where_ref[0] + rows_ref[first + q]]
            total = k_ref[q, j].astype(F32) + product[q * v : (q + 1) * v].astype(F32) + ct_ref[q, j].astype(F32)
            o_ref[q, j] = total / (base - occ_ref[where_ref[1] + where_ref[3] + j])
        return carry

    lax.fori_loop(0, width, column, 0)


def joined(wp, parts, chunk, ct, k, tall, wide, occ, where, rows, into):
    width, _, v, _ = parts[0].shape
    depth, steps = wp.shape[2], rows.shape[0] // width
    where = jnp.concatenate([where, jnp.full((1,), chunk * width, I32)])
    block = (width, width, v, v)
    by_row = pl.BlockSpec(block, lambda n, rows, where: (rows[n * width] // width, chunk, 0, 0))
    return pl.pallas_call(
        functools.partial(joined_kernel, len(parts)),
        out_shape=jax.ShapeDtypeStruct(into.shape, into.dtype),
        grid_spec=pltpu.PrefetchScalarGridSpec(
            num_scalar_prefetch=2,
            grid=(steps,),
            in_specs=[pl.BlockSpec(memory_space=pltpu.SMEM), resident(tall.shape), resident(wide.shape)]
            + [pl.BlockSpec(memory_space=pl.ANY)]
            + [
                pl.BlockSpec((1, v, depth), lambda n, rows, where, q=q: (rows[n * width + q], 0, 0))
                for q in range(width)
            ]
            + [resident(p.shape) for p in parts]
            + [pl.BlockSpec(block, lambda n, rows, where: (n, 0, 0, 0)), by_row],
            out_specs=by_row,
        ),
        input_output_aliases={5: 0},
        compiler_params=params(),
        cost_estimate=cost(2 * steps * width**2 * v * v * depth, 2 * steps * width * v * (depth + 4 * width * v)),
        name="joined",
    )(rows, where, occ, tall, wide, into, *[wp] * width, *parts, ct, k)


class Links:
    def __init__(self, groups, jgroups):
        self.groups, self.jgroups, self.ratio = groups, jgroups, jgroups // groups

    def near(self, x, s):
        return lax.ppermute(x, "igrp", [(i, i ^ s) for i in range(self.groups)])

    def route(self, x, s):
        pairs = [
            (i * self.jgroups + z * self.ratio + y, z * self.jgroups + (i ^ s) * self.ratio + y)
            for i in range(self.groups)
            for z in range(self.groups)
            for y in range(self.ratio)
        ]
        return lax.ppermute(x, AXES, pairs)

    def swap(self, x, d):
        return lax.ppermute(x, "jgrp", [(j, j ^ d) for j in range(self.jgroups)])

    def spread(self, w, held, bit):
        pairs = [
            ((z ^ held) * self.jgroups + z * self.ratio + y, (z ^ held ^ bit) * self.jgroups + z * self.ratio + y)
            for z in range(self.groups)
            for y in range(self.ratio)
        ]
        return lax.ppermute(w, AXES, pairs)

    def bits(self):
        bit, found = self.groups // 2, []
        while bit:
            found.append(bit)
            bit //= 2
        return found


def exchange(links, mine, near, far, window, rider=None):
    groups, chunks = links.groups, range(len(near))
    sides = [list(range(p, groups, 2)) for p in range(2)]
    steps = [(h, side) for h in chunks for side in sides]
    plan = [[] for _ in range(len(steps) + 1)]
    for h in chunks:
        for s in range(1, groups):
            at = 2 * h + s % 2 if s > 1 else h * len(steps) if rider is not None or h else 1
            plan[min(at, len(steps))].append((h, s))
    earlier, before = [], []
    for t in range(len(steps) + 1):
        slots = []
        if t < len(steps):
            h, side = steps[t]
            slots += [(mine[h], s) for s in side]
        if t > 0:
            back, back_side = steps[t - 1]
            slots += [(far[0][back], s) for s in back_side]
        for g, s in plan[t]:
            if not any(x is mine[g] and n == s for x, n in slots):
                slots.append((mine[g], s))
        arrays = [x[n] for x, n in slots]
        riding = rider is not None and t == len(steps)
        if riding:
            arrays.append(rider[0])
        if earlier:
            arrays = tie(arrays, earlier)
        for (x, n), array in zip(slots, arrays):
            x[n] = array
        earlier = []
        if t < len(steps):
            for s in side:
                far[0][h][s] = links.route(mine[h][s], s)
                earlier.append(far[0][h][s])
        if t > 0:
            for d in range(1, links.ratio):
                for s in back_side:
                    far[d][back][s] = links.swap(far[0][back][s], d)
                    earlier.append(far[d][back][s])
        for g, s in plan[t]:
            near[g][s] = links.near(mine[g][s], s)
            earlier.append(near[g][s])
        for g in chunks:
            near[g][0] = mine[g][0]
        earlier, before = earlier + window(t, before), earlier
        if riding:
            earlier.append(rider[1](arrays[-1]))
    return earlier


def body(t_start, integrals, weights, neighbours, eps_occ, eps_vir):
    row_count, cols, v, _ = t_start.shape
    groups, jgroups = lax.axis_size("igrp"), lax.axis_size("jgrp")
    links = Links(groups, jgroups)
    ratio = links.ratio
    my_i, my_j = lax.axis_index("igrp"), lax.axis_index("jgrp")
    my_z, my_half = my_j // ratio, my_j % ratio
    width = cols // 2
    chunks = range(2)
    sides = [list(range(p, groups, 2)) for p in range(2)]

    lists = listed_offsets(neighbours, groups, row_count)
    slots = relative_slots(neighbours, lists, groups, row_count)
    asked = lax.dynamic_slice_in_dim(lists, my_i, 1, 1)[:, 0]
    order = my_i ^ jnp.arange(groups, dtype=I32)
    rows = jnp.sum(
        asked[None] * (jnp.arange(groups, dtype=I32)[None, :, None] == order[:, None, None]).astype(I32), axis=1
    ).reshape(-1)
    every_row = jnp.arange(row_count, dtype=I32)
    where = jnp.stack([my_i * row_count, my_j * cols, my_half]).astype(I32)
    tall, wide = eps_vir.reshape(v, 1), eps_vir.reshape(1, v)

    def slots_of(first, count):
        return lax.dynamic_slice_in_dim(slots, first, count, 0)

    def empty():
        return [[None] * groups for _ in chunks], [[[None] * groups for _ in chunks] for _ in range(ratio)]

    made = {}

    def opening(t, earlier):
        if t == 0:
            made["wp"] = slotted([weights], jnp.zeros((), I32), slots_of(my_i * row_count, row_count), groups)
            return [made["wp"]]
        if t in (2, 4):
            made["c", t // 2 - 1] = direct(made["wp"], rows, near[t // 2 - 1])
            return [made["c", t // 2 - 1]]
        return []

    bits = links.bits()

    def deliver(h, w, far_side):
        there = {0: w, bits[0]: far_side}
        for bit in bits[1:]:
            for held in list(there):
                there[held ^ bit] = links.spread(there[held], held, bit)
        sources = [there[n] for n in range(groups)]
        return slotted(sources, my_i ^ my_z, slots_of(my_j * cols + h * width, width), groups)

    own_w = [lax.dynamic_slice_in_dim(weights, my_half * cols + h * width, width, 0) for h in chunks]
    mine = [[*pick_rows(t_start, rows, groups, width, h)] for h in chunks]
    near, far = empty()
    last = exchange(links, mine, near, far, opening, (own_w[0], lambda w: links.spread(w, 0, bits[0])))
    came, second = tie([last.pop(), own_w[1]], last)
    second_came = links.spread(second, 0, bits[0])
    wpj = [deliver(0, own_w[0], came), None]

    def rows_of(h, halves):
        return jnp.concatenate(
            [(my_half ^ d) * cols + h * width + jnp.arange(width, dtype=I32) for d in halves]
        )

    chosen = ((rows // cols) ^ my_half) * len(chunks) + (rows % cols) // width

    def listed_rows(h, c):
        ready = [None] * groups
        for side in [[*range(p, groups, 2)] for p in range(2)] if h == 0 else [[*range(groups)]]:
            which = jnp.asarray([s * CAP + n for s in side for n in range(CAP)], I32)
            some = finish(
                wpj, [c], which, [h], integrals, tall, wide, eps_occ, where,
                jnp.concatenate([rows[s * CAP : (s + 1) * CAP] for s in side]),
                jnp.concatenate([chosen[s * CAP : (s + 1) * CAP] for s in side]),
                [piece for half in far_now for piece in half],
                [jax.ShapeDtypeStruct((width, CAP, v, v), BF16)] * len(side),
            )
            for s, x in zip(side, some):
                ready[s] = x
        return ready

    for sweep in range(ITERS - 1):
        c = [made["c", h] if sweep == 0 else direct(made["wp"], rows, near[h]) for h in chunks]
        far_now = far
        mine = [listed_rows(0, c[0]), [None] * groups]
        near, far = empty()
        final = sweep == ITERS - 2
        state = {}
        every, first_half = range(ratio), jnp.zeros((width,), I32)

        def complete(over, h, halves):
            some_rows = rows_of(h, halves)
            use = jnp.repeat(jnp.arange(len(halves), dtype=I32), width)
            [state["out"]] = finish(
                wpj, [state["c", n] for n in over], some_rows, over, integrals, tall, wide, eps_occ, where, some_rows,
                use, [far[d][h] for d in halves], [jax.ShapeDtypeStruct((row_count, cols, v, v), F32)], state.get("out"),
            )
            return state["out"]

        def middle(t, earlier):
            if t == 1:
                if wpj[1] is None:
                    arrived, held_rows = tie([second_came, second], earlier + mine[0][1::2])
                    wpj[1] = deliver(1, held_rows, arrived)
                mine[1][:] = listed_rows(1, c[1])
                return mine[1]
            if t == 0 or not final:
                return []
            if t == 2:
                state["c", 0] = direct(made["wp"], every_row, near[0])
                return [state["c", 0]]
            if t == 3:
                some_rows = rows_of(0, every)
                use = jnp.repeat(jnp.arange(ratio, dtype=I32), width)
                [state["ct"]] = finish(
                    wpj, None, some_rows, [1], integrals, tall, wide, eps_occ, where, some_rows, use,
                    [far[d][0] for d in every],
                    [jax.ShapeDtypeStruct((ratio * width, width, v, v), BF16)],
                )
                return [state["ct"], complete([0], 0, every)]
            return []

        exchange(links, mine, near, far, middle)
    state["c", 1] = direct(made["wp"], rows_of(1, every), near[1], placed=True)
    complete([0, 1], 1, [0])
    state["out"] = joined(
        made["wp"], near[1], 1, state["ct"], integrals, tall, wide, eps_occ, where, rows_of(0, every), state["out"]
    )
    for d in every[1:]:
        complete([0, 1], 1, [d])
    return state["out"]


def solution(mesh):
    placed = (
        P("igrp", "jgrp", None, None),
        P("igrp", "jgrp", None, None),
        P("igrp", None, None, None),
        P(),
        P(),
        P(),
    )
    return jax.shard_map(
        body, mesh=mesh, in_specs=placed, out_specs=P("igrp", "jgrp", None, None), check_vma=False
    )
```
